32 devices in a mesh: win: 2 (over y), wide: 4 (over x, core), narrow: 4 (over z).
Axes of the slice: x: 2, y: 2, z: 4, core: 2. Of those that a mesh axis runs over, the one named last changes fastest.
Arguments:
- spectra: bfloat16 [64, 2, 128, 4096], P('win', None, 'wide', 'narrow'), parts along dimension 0, may hold values from -6 to 6
- live: int32 [256], P(('win', 'wide')), parts along dimension 0, may hold values 0 or 1
Outputs:
- correlation: float32 [512, 128, 128], P(('win', 'narrow'), 'wide'), parts along dimension 0
The draws below stay inside these ranges and needn't reach their ends.
There are 2 independent parts, one for each index of `win`. The reference program is written for one: setup_inputs(seed, part) draws one part's arguments, and reference() takes and returns one part's arrays. A program takes and returns all parts, laid end to end along the dimension named above; each array names one. Nothing has to cross between parts.
All inputs are finite; a program needn't handle non-finite values. No bound on the sum of `live` on one device may be relied on, other than what follows from the above.
Results may differ from the reference program's by a relative error of at most 0.0085.
Values may be sent and summed in bfloat16 or wider, within the bound.
A program may use at most 256 MiB of HBM per device.

```python
import math
import jax
import jax.numpy as jnp
from jax import lax

F = 4096
L = 256
K = 4
S = 32
BLK = 32
C = 128
N_WIDE = 4
N_NARROW = 4


def place_ends(entries, key, low, top_value):
    index_at = [jax.random.randint(jax.random.fold_in(key, axis), (), 0, length) for axis, length in enumerate(entries.shape)]
    main_axis = entries.shape.index(max(entries.shape))
    next_to = index_at[:main_axis] + [(index_at[main_axis] + 1) % entries.shape[main_axis]] + index_at[main_axis + 1:]
    return entries.at[tuple(index_at)].set(low).at[tuple(next_to)].set(top_value)


def block_levels(stream_key, extent, shards, least, high):
    def one(dim, parts):
        steps = jax.random.uniform(jax.random.fold_in(jax.random.fold_in(stream_key, 6), dim), (parts,), jnp.float32, least / len(shards), high / len(shards))
        return jnp.repeat(jnp.exp(steps), extent[dim] // parts).reshape((-1,) + (1,) * (len(extent) - dim - 1))

    loudness = one(*shards[0])
    for cut in shards[1:]:
        loudness = loudness * one(*cut)
    return loudness


def scatter_about(stream_key, extent, scale, most, shards=(), kind=jnp.bfloat16):
    gain = block_levels(stream_key, extent, shards, -0.22, 0.18) if shards else 1.0
    result = jax.random.normal(stream_key, extent, jnp.float32) * scale * gain
    return jnp.minimum(jnp.maximum(result, -most), most).astype(kind)


def setup_inputs(seed: int = 0, part: int = 0) -> dict:
    keys = jax.random.split(jax.random.key(seed), 3)
    own_keys = jax.random.split(jax.random.fold_in(keys[2], part), 3)
    spectra = scatter_about(own_keys[0], (S, 2, C, F), 1.0, 6.0, ((2, 4), (3, 4)))
    live = place_ends((jax.random.randint(own_keys[1], (C,), 0, 8) < 7).astype(jnp.int32), jax.random.fold_in(own_keys[1], 1), 0, 1)
    return dict(spectra=spectra, live=live)


def reference(spectra, live):
    band_size = K * BLK
    group_bins = F // N_NARROW
    padded = jnp.pad(spectra, ((0, 0), (0, 0), (0, band_size), (0, 0)))
    live_padded = jnp.pad(live, (0, band_size))
    bin_index = jnp.arange(F, dtype=jnp.int32)
    lag_shift = jnp.arange(L, dtype=jnp.int32) - L // 2
    phase_angle = jnp.mod(bin_index[:, None] * lag_shift[None, :], F).astype(jnp.float32) * jnp.float32(2.0 * math.pi / F)
    cos_table = jnp.cos(phase_angle)
    sin_table = jnp.sin(phase_angle)
    high = lax.Precision.HIGHEST

    def one_block(block_index):
        first_row = (block_index * BLK).astype(jnp.int32)
        row_block = lax.dynamic_slice_in_dim(padded, first_row, BLK, 2).astype(jnp.float32)
        partner_block = lax.dynamic_slice_in_dim(padded, first_row, band_size, 2).astype(jnp.float32)
        live_rows = lax.dynamic_slice_in_dim(live_padded, first_row, BLK, 0)
        live_partner = lax.dynamic_slice_in_dim(live_padded, first_row, band_size, 0)
        row_ids = first_row + jnp.arange(BLK, dtype=jnp.int32)
        partner_ids = first_row + jnp.arange(band_size, dtype=jnp.int32)
        keep_mask = ((row_ids[:, None] != partner_ids[None, :]) & (live_rows[:, None] > 0) & (live_partner[None, :] > 0)).astype(jnp.float32)
        stack_scale = keep_mask[:, :, None] / jnp.float32(math.sqrt(S))
        real_sum = jnp.einsum('scif,scjf->ijf', row_block, partner_block, precision=high)
        imag_sum = jnp.einsum('sif,sjf->ijf', row_block[:, 0], partner_block[:, 1], precision=high) - jnp.einsum('sif,sjf->ijf', row_block[:, 1], partner_block[:, 0], precision=high)
        cross_real = (real_sum * stack_scale).astype(jnp.bfloat16).astype(jnp.float32)
        cross_imag = (imag_sum * stack_scale).astype(jnp.bfloat16).astype(jnp.float32)

        def add_group(total, group_index):
            first_bin = (group_index * group_bins).astype(jnp.int32)
            real_part = lax.dynamic_slice_in_dim(cross_real, first_bin, group_bins, 2)
            imag_part = lax.dynamic_slice_in_dim(cross_imag, first_bin, group_bins, 2)
            cos_part = lax.dynamic_slice_in_dim(cos_table, first_bin, group_bins, 0)
            sin_part = lax.dynamic_slice_in_dim(sin_table, first_bin, group_bins, 0)
            partial_sum = jnp.einsum('ijf,ft->tij', real_part, cos_part, precision=high) - jnp.einsum('ijf,ft->tij', imag_part, sin_part, precision=high)
            rounded = lax.optimization_barrier((partial_sum / jnp.float32(math.sqrt(F))).astype(jnp.bfloat16))
            return (total + rounded.astype(jnp.float32), None)
        start_total = jnp.zeros((L, BLK, band_size), jnp.float32)
        lag_values, unused = lax.scan(add_group, start_total, jnp.arange(N_NARROW, dtype=jnp.int32))
        return lag_values
    blocks = lax.map(one_block, jnp.arange(N_WIDE, dtype=jnp.int32))
    return jnp.transpose(blocks, (1, 0, 2, 3)).reshape(L, N_WIDE * BLK, band_size)
```

```python
import functools
import math

import jax
import jax.numpy as jnp
from jax import lax
from jax.experimental import pallas as pl
from jax.experimental.pallas import tpu as pltpu
from jax.sharding import PartitionSpec as P

F = 4096
L = 256
K = 4
S = 32
BINS = 128


def from_behind(array, axis, by):
    length = lax.axis_size(axis)
    pairs = [(i, i + by) for i in range(length) if 0 <= i + by < length]
    return lax.ppermute(array, axis, pairs)


def any_width(spectra, live):
    block_size = spectra.shape[2]
    bins_here = spectra.shape[3]
    wide_pos = lax.axis_index("wide")
    narrow_pos = lax.axis_index("narrow")
    high = lax.Precision.HIGHEST
    spectra_list = [spectra]
    live_list = [live]
    for offset_step in range(1, K):
        received = from_behind((spectra, live), "wide", -offset_step)
        spectra_list.append(received[0])
        live_list.append(received[1])
    partners = jnp.concatenate(spectra_list, axis=2)
    partner_live = jnp.concatenate(live_list, axis=0)
    band_size = partners.shape[2]
    real_sum = jnp.einsum("scif,scjf->ijf", spectra, partners, preferred_element_type=jnp.float32)
    imag_sum = jnp.einsum(
        "sif,sjf->ijf", spectra[:, 0], partners[:, 1], preferred_element_type=jnp.float32
    ) - jnp.einsum(
        "sif,sjf->ijf", spectra[:, 1], partners[:, 0], preferred_element_type=jnp.float32
    )
    row_ids = wide_pos * block_size + jnp.arange(block_size, dtype=jnp.int32)
    partner_ids = wide_pos * block_size + jnp.arange(band_size, dtype=jnp.int32)
    keep_mask = (
        (row_ids[:, None] != partner_ids[None, :])
        & (live[:, None] > 0)
        & (partner_live[None, :] > 0)
    ).astype(jnp.float32)
    stack_scale = keep_mask[:, :, None] / jnp.float32(math.sqrt(S))
    cross_real = (real_sum * stack_scale).astype(jnp.bfloat16)
    cross_imag = (imag_sum * stack_scale).astype(jnp.bfloat16)
    lag_shift = jnp.arange(L, dtype=jnp.int32) - L // 2
    bin_index = narrow_pos * bins_here + jnp.arange(bins_here, dtype=jnp.int32)
    phase_angle = jnp.mod(bin_index[:, None] * lag_shift[None, :], F).astype(
        jnp.float32
    ) * jnp.float32(2.0 * math.pi / F)
    cos_table = jnp.cos(phase_angle)
    sin_table = jnp.sin(phase_angle)
    summed = jnp.einsum(
        "ijf,ft->tij", cross_real, cos_table, precision=high, preferred_element_type=jnp.float32
    ) - jnp.einsum(
        "ijf,ft->tij", cross_imag, sin_table, precision=high, preferred_element_type=jnp.float32
    )
    return lax.psum_scatter(
        (summed / jnp.float32(math.sqrt(F))).astype(jnp.bfloat16),
        "narrow",
        scatter_dimension=0,
        tiled=True,
    ).astype(jnp.float32)


def correlate_kernel(crossing, meta_ref, *refs):
    if crossing:
        own, near, far_a, far_b, table, before, out, acc, spread, gram = refs
        sources = (own, near, far_a, far_b)
    else:
        own, near, table, out, spread, gram = refs
        acc = out
        sources = (own, near)
    step = pl.program_id(0)
    points = 32 * len(sources)

    @pl.when(step == 0)
    def _():
        if crossing:
            acc[...] = before[...]
        else:
            acc[...] = jnp.zeros_like(acc)
            spread[...] = jnp.zeros_like(spread)

    def turn(s, carry):
        for c in range(2):
            tile = jnp.concatenate([ref[s, c] for ref in sources], axis=0)
            turned = tile.astype(jnp.float32).T
            spread[pl.ds(pl.multiple_of((c * S + s) * BINS, BINS), BINS), 0:points] = turned
        return carry

    lax.fori_loop(0, S, turn, 0, unroll=4)

    def one_bin(f, carry):
        both = spread[pl.ds(f, 2 * S, stride=BINS), :]
        a, b = both[:S], both[S:]
        plain = both.astype(jnp.bfloat16)
        crossed = jnp.concatenate([b, -a], axis=0).astype(jnp.bfloat16)
        right = jnp.concatenate([plain, crossed], axis=1)
        product = lax.dot_general(
            plain[:, :32], right, (((0,), (0,)), ((), ())), preferred_element_type=jnp.float32
        )
        gram[pl.ds(pl.multiple_of(f * 32, 32), 32), :] = product[:, :128]
        gram[pl.ds(pl.multiple_of((BINS + f) * 32, 32), 32), :] = product[:, 128:]
        return carry

    lax.fori_loop(0, BINS, one_bin, 0, unroll=8)

    lane = lax.broadcasted_iota(jnp.int32, (1, 128), 1)
    sign = jnp.where((lane >= 64) & (meta_ref[1] == 1), -1.0, 1.0).astype(jnp.float32)

    def two_rows(ip, carry):
        real = [gram[pl.ds(2 * ip + r, BINS, stride=32), :] for r in range(2)]
        imag = [gram[pl.ds(BINS * 32 + 2 * ip + r, BINS, stride=32), :] * sign for r in range(2)]
        top = jnp.concatenate(real, axis=1)
        low = jnp.concatenate(imag, axis=1)
        right = jnp.concatenate([top, low], axis=0).astype(jnp.bfloat16)
        cols = pl.ds(pl.multiple_of(ip * 256, 256), 256)
        acc[:, cols] += jnp.dot(table[0], right, preferred_element_type=jnp.float32)
        return carry

    lax.fori_loop(0, 16, two_rows, 0, unroll=2)

    if crossing:
        @pl.when(step == pl.num_programs(0) - 1)
        def _():
            out[...] = (acc[...] * (1.0 / math.sqrt(S * F))).astype(out.dtype)


def correlate(meta, own, near, far, table, before):
    crossing = far is not None
    half = own.shape[3] // BINS // 2
    block = (S, 2, 32, BINS)
    placed = pl.BlockSpec(block, lambda k, m: (0, 0, 0, m[0] + k))
    near_by = pl.BlockSpec(block, lambda k, m: (0, 0, 0, k))
    table_spec = pl.BlockSpec((1, L, 2 * BINS), lambda k, m: (m[0] + k, 0, 0))
    whole = pl.BlockSpec((L, 4096), lambda k, m: (0, 0))
    scratch = [pltpu.VMEM((2 * S * BINS, 128), jnp.float32), pltpu.VMEM((2 * BINS * 32, 128), jnp.float32)]
    if crossing:
        in_specs = [placed, placed, near_by, near_by, table_spec, whole]
        operands = (own, near, far[0], far[1], table, before)
        scratch = [pltpu.VMEM((L, 4096), jnp.float32)] + scratch
    else:
        in_specs = [placed, placed, table_spec]
        operands = (own, near, table)
    return pl.pallas_call(
        functools.partial(correlate_kernel, crossing),
        out_shape=jax.ShapeDtypeStruct((L, 4096), jnp.bfloat16 if crossing else jnp.float32),
        grid_spec=pltpu.PrefetchScalarGridSpec(
            num_scalar_prefetch=1, grid=(half,), in_specs=in_specs, out_specs=whole, scratch_shapes=scratch
        ),
        compiler_params=pltpu.CompilerParams(vmem_limit_bytes=48 * 2**20),
        cost_estimate=pl.CostEstimate(flops=2 * 10**10, bytes_accessed=2**23, transcendentals=0),
    )(meta, *operands)


def two_chips(spectra, live):
    bins_here = spectra.shape[3]
    half = bins_here // 2
    wide_pos = lax.axis_index("wide")
    narrow_pos = lax.axis_index("narrow")
    x, core = wide_pos // 2, wide_pos % 2
    over_x = [(0, 2), (1, 3), (2, 0), (3, 1)]
    on_chip = [(0, 1), (1, 0), (2, 3), (3, 2)]
    leaving = lax.dynamic_slice_in_dim(spectra, (1 - x) * half, half, 3)
    far_a = lax.ppermute(leaving, "wide", over_x)
    near = lax.ppermute(spectra, "wide", on_chip)
    far_b = lax.ppermute(far_a, "wide", on_chip)
    all_live = lax.all_gather(live, "wide", tiled=True)

    lag_shift = jnp.arange(L, dtype=jnp.int32) - L // 2
    bin_index = narrow_pos * bins_here + jnp.arange(bins_here, dtype=jnp.int32)
    bin_index = bin_index.reshape(-1, 1, BINS)
    angle = jnp.mod(bin_index * lag_shift[None, :, None], F).astype(jnp.float32) * jnp.float32(
        2.0 * math.pi / F
    )
    table = jnp.concatenate([jnp.cos(angle), -jnp.sin(angle)], axis=2).astype(jnp.bfloat16)

    chunks = half // BINS
    first = jnp.stack([(1 - x) * chunks, x]).astype(jnp.int32)
    second = jnp.stack([x * chunks, x]).astype(jnp.int32)
    before = correlate(first, spectra, near, None, table, None)
    partial = correlate(second, spectra, near, (far_a, far_b), table, before)
    mine = lax.psum_scatter(partial, "narrow", scatter_dimension=0, tiled=True)
    mine = mine.reshape(-1, 32, 128)
    back_a = lax.ppermute(mine[:, :, 64:96], "wide", [(2, 0), (3, 1)])
    back_b = lax.ppermute(mine[:, :, 96:], "wide", [(2, 1), (3, 0)])
    mine = mine.astype(jnp.float32)
    far_1 = mine[:, :, 64:96] + jnp.swapaxes(back_a, 1, 2).astype(jnp.float32)
    far_2 = mine[:, :, 96:] + jnp.swapaxes(back_b, 1, 2).astype(jnp.float32)
    q1 = jnp.where(core == 0, mine[:, :, 32:64], far_2)
    stacked = jnp.concatenate([mine[:, :, :32], q1, far_1, far_2], axis=2)
    row = wide_pos * 32 + jnp.arange(32, dtype=jnp.int32)
    partner = wide_pos * 32 + jnp.arange(128, dtype=jnp.int32)
    partner_live = lax.dynamic_slice_in_dim(jnp.pad(all_live, (0, 128)), wide_pos * 32, 128)
    keep = (
        (row[:, None] != partner[None, :])
        & (live[:, None] > 0)
        & (partner_live[None, :] > 0)
        & (partner[None, :] < 128)
    )
    return jnp.where(keep[None], stacked, 0.0)


def solution(mesh):
    placed = (P("win", None, "wide", "narrow"), P(("win", "wide")))
    fits = mesh.shape["wide"] == 4 and mesh.shape["narrow"] == 4
    return jax.shard_map(
        two_chips if fits else any_width,
        mesh=mesh,
        in_specs=placed,
        out_specs=P(("win", "narrow"), "wide", None),
        check_vma=False,
    )
```

```python
import functools
import math

import jax
import jax.numpy as jnp
from jax import lax
from jax.experimental import pallas as pl
from jax.experimental.pallas import tpu as pltpu
from jax.sharding import PartitionSpec as P

F = 4096
L = 256
K = 4
S = 32
BINS = 128


def from_behind(array, axis, by):
    length = lax.axis_size(axis)
    pairs = [(i, i + by) for i in range(length) if 0 <= i + by < length]
    return lax.ppermute(array, axis, pairs)


def any_width(spectra, live):
    block_size = spectra.shape[2]
    bins_here = spectra.shape[3]
    wide_pos = lax.axis_index("wide")
    narrow_pos = lax.axis_index("narrow")
    high = lax.Precision.HIGHEST
    spectra_list = [spectra]
    live_list = [live]
    for offset_step in range(1, K):
        received = from_behind((spectra, live), "wide", -offset_step)
        spectra_list.append(received[0])
        live_list.append(received[1])
    partners = jnp.concatenate(spectra_list, axis=2)
    partner_live = jnp.concatenate(live_list, axis=0)
    band_size = partners.shape[2]
    real_sum = jnp.einsum("scif,scjf->ijf", spectra, partners, preferred_element_type=jnp.float32)
    imag_sum = jnp.einsum(
        "sif,sjf->ijf", spectra[:, 0], partners[:, 1], preferred_element_type=jnp.float32
    ) - jnp.einsum(
        "sif,sjf->ijf", spectra[:, 1], partners[:, 0], preferred_element_type=jnp.float32
    )
    row_ids = wide_pos * block_size + jnp.arange(block_size, dtype=jnp.int32)
    partner_ids = wide_pos * block_size + jnp.arange(band_size, dtype=jnp.int32)
    keep_mask = (
        (row_ids[:, None] != partner_ids[None, :])
        & (live[:, None] > 0)
        & (partner_live[None, :] > 0)
    ).astype(jnp.float32)
    stack_scale = keep_mask[:, :, None] / jnp.float32(math.sqrt(S))
    cross_real = (real_sum * stack_scale).astype(jnp.bfloat16)
    cross_imag = (imag_sum * stack_scale).astype(jnp.bfloat16)
    lag_shift = jnp.arange(L, dtype=jnp.int32) - L // 2
    bin_index = narrow_pos * bins_here + jnp.arange(bins_here, dtype=jnp.int32)
    phase_angle = jnp.mod(bin_index[:, None] * lag_shift[None, :], F).astype(
        jnp.float32
    ) * jnp.float32(2.0 * math.pi / F)
    cos_table = jnp.cos(phase_angle)
    sin_table = jnp.sin(phase_angle)
    summed = jnp.einsum(
        "ijf,ft->tij", cross_real, cos_table, precision=high, preferred_element_type=jnp.float32
    ) - jnp.einsum(
        "ijf,ft->tij", cross_imag, sin_table, precision=high, preferred_element_type=jnp.float32
    )
    return lax.psum_scatter(
        (summed / jnp.float32(math.sqrt(F))).astype(jnp.bfloat16),
        "narrow",
        scatter_dimension=0,
        tiled=True,
    ).astype(jnp.float32)


def correlate_kernel(crossing, meta_ref, *refs):
    if crossing:
        own, near, far_a, far_b, table, before, out, acc, spread, gram = refs
        sources = (own, near, far_a, far_b)
    else:
        own, near, table, out, spread, gram = refs
        acc = out
        sources = (own, near)
    step = pl.program_id(0)
    points = 32 * len(sources)

    @pl.when(step == 0)
    def _():
        if crossing:
            acc[...] = before[...]
        else:
            acc[...] = jnp.zeros_like(acc)
            spread[...] = jnp.zeros_like(spread)

    def turn(s, carry):
        for c in range(2):
            tile = jnp.concatenate([ref[s, c] for ref in sources], axis=0)
            turned = tile.astype(jnp.float32).T
            spread[pl.ds(pl.multiple_of((c * S + s) * BINS, BINS), BINS), 0:points] = turned
        return carry

    lax.fori_loop(0, S, turn, 0, unroll=4)

    def one_bin(f, carry):
        both = spread[pl.ds(f, 2 * S, stride=BINS), :]
        a, b = both[:S], both[S:]
        plain = both.astype(jnp.bfloat16)
        crossed = jnp.concatenate([b, -a], axis=0).astype(jnp.bfloat16)
        right = jnp.concatenate([plain, crossed], axis=1)
        product = lax.dot_general(
            plain[:, :32], right, (((0,), (0,)), ((), ())), preferred_element_type=jnp.float32
        )
        gram[pl.ds(pl.multiple_of(f * 32, 32), 32), :] = product[:, :128]
        gram[pl.ds(pl.multiple_of((BINS + f) * 32, 32), 32), :] = product[:, 128:]
        return carry

    lax.fori_loop(0, BINS, one_bin, 0, unroll=8)

    lane = lax.broadcasted_iota(jnp.int32, (1, 128), 1)
    sign = jnp.where((lane >= 64) & (meta_ref[1] == 1), -1.0, 1.0).astype(jnp.float32)

    def two_rows(ip, carry):
        real = [gram[pl.ds(2 * ip + r, BINS, stride=32), :] for r in range(2)]
        imag = [gram[pl.ds(BINS * 32 + 2 * ip + r, BINS, stride=32), :] * sign for r in range(2)]
        top = jnp.concatenate(real, axis=1)
        low = jnp.concatenate(imag, axis=1)
        right = jnp.concatenate([top, low], axis=0).astype(jnp.bfloat16)
        cols = pl.ds(pl.multiple_of(ip * 256, 256), 256)
        acc[:, cols] += jnp.dot(table[0], right, preferred_element_type=jnp.float32)
        return carry

    lax.fori_loop(0, 16, two_rows, 0, unroll=2)

    if crossing:
        @pl.when(step == pl.num_programs(0) - 1)
        def _():
            out[...] = (acc[...] * (1.0 / math.sqrt(S * F))).astype(out.dtype)


def correlate(meta, own, near, far, table, before):
    crossing = far is not None
    half = own.shape[3] // BINS // 2
    block = (S, 2, 32, BINS)
    placed = pl.BlockSpec(block, lambda k, m: (0, 0, 0, m[0] + k))
    near_by = pl.BlockSpec(block, lambda k, m: (0, 0, 0, k))
    table_spec = pl.BlockSpec((1, L, 2 * BINS), lambda k, m: (m[0] + k, 0, 0))
    whole = pl.BlockSpec((L, 4096), lambda k, m: (0, 0))
    scratch = [pltpu.VMEM((2 * S * BINS, 128), jnp.float32), pltpu.VMEM((2 * BINS * 32, 128), jnp.float32)]
    if crossing:
        in_specs = [placed, near_by, near_by, near_by, table_spec, whole]
        operands = (own, near, far[0], far[1], table, before)
        scratch = [pltpu.VMEM((L, 4096), jnp.float32)] + scratch
    else:
        in_specs = [placed, near_by, table_spec]
        operands = (own, near, table)
    return pl.pallas_call(
        functools.partial(correlate_kernel, crossing),
        out_shape=jax.ShapeDtypeStruct((L, 4096), jnp.bfloat16 if crossing else jnp.float32),
        grid_spec=pltpu.PrefetchScalarGridSpec(
            num_scalar_prefetch=1, grid=(half,), in_specs=in_specs, out_specs=whole, scratch_shapes=scratch
        ),
        compiler_params=pltpu.CompilerParams(vmem_limit_bytes=48 * 2**20),
        cost_estimate=pl.CostEstimate(flops=2 * 10**10, bytes_accessed=2**23, transcendentals=0),
    )(meta, *operands)


def fold(lags):
    return jnp.concatenate(jnp.split(lags, 4, axis=0), axis=2)


def unfold(folded):
    return jnp.concatenate(jnp.split(folded, 4, axis=2), axis=0)


def two_chips(spectra, live):
    bins_here = spectra.shape[3]
    half = bins_here // 2
    wide_pos = lax.axis_index("wide")
    narrow_pos = lax.axis_index("narrow")
    x, core = wide_pos // 2, wide_pos % 2
    over_x = [(0, 2), (1, 3), (2, 0), (3, 1)]
    on_chip = [(0, 1), (1, 0), (2, 3), (3, 2)]
    leaving = lax.dynamic_slice_in_dim(spectra, (1 - x) * half, half, 3)
    staying = lax.dynamic_slice_in_dim(spectra, x * half, half, 3)
    far_a = lax.ppermute(leaving, "wide", over_x)
    near_first = lax.ppermute(leaving, "wide", on_chip)
    near_second = lax.ppermute(staying, "wide", on_chip)
    far_b = lax.ppermute(far_a, "wide", on_chip)
    live_near = lax.ppermute(live, "wide", on_chip)
    live_a = lax.ppermute(live, "wide", over_x)
    live_b = lax.ppermute(live_a, "wide", on_chip)

    lag_shift = jnp.arange(L, dtype=jnp.int32) - L // 2
    bin_index = narrow_pos * bins_here + jnp.arange(bins_here, dtype=jnp.int32)
    bin_index = bin_index.reshape(-1, 1, BINS)
    angle = jnp.mod(bin_index * lag_shift[None, :, None], F).astype(jnp.float32) * jnp.float32(
        2.0 * math.pi / F
    )
    table = jnp.concatenate([jnp.cos(angle), -jnp.sin(angle)], axis=2).astype(jnp.bfloat16)

    chunks = half // BINS
    first = jnp.stack([(1 - x) * chunks, x]).astype(jnp.int32)
    second = jnp.stack([x * chunks, x]).astype(jnp.int32)
    before = correlate(first, spectra, near_first, None, table, None)
    partial = correlate(second, spectra, near_second, (far_a, far_b), table, before)
    mine = lax.psum_scatter(partial, "narrow", scatter_dimension=0, tiled=True)
    mine = mine.reshape(-1, 32, 128)
    back_a = unfold(lax.ppermute(fold(mine[:, :, 64:96]), "wide", [(2, 0), (3, 1)]))
    back_b = unfold(lax.ppermute(fold(mine[:, :, 96:]), "wide", [(2, 1), (3, 0)]))
    mine = mine.astype(jnp.float32)
    far_1 = mine[:, :, 64:96] + jnp.swapaxes(back_a, 1, 2).astype(jnp.float32)
    far_2 = mine[:, :, 96:] + jnp.swapaxes(back_b, 1, 2).astype(jnp.float32)
    q1 = jnp.where(core == 0, mine[:, :, 32:64], far_2)
    stacked = jnp.concatenate([mine[:, :, :32], q1, far_1, far_2], axis=2)
    row = wide_pos * 32 + jnp.arange(32, dtype=jnp.int32)
    partner = wide_pos * 32 + jnp.arange(128, dtype=jnp.int32)
    partner_live = jnp.concatenate([live, jnp.where(core == 0, live_near, live_b), live_a, live_b])
    keep = (
        (row[:, None] != partner[None, :])
        & (live[:, None] > 0)
        & (partner_live[None, :] > 0)
        & (partner[None, :] < 128)
    )
    return jnp.where(keep[None], stacked, 0.0)


def solution(mesh):
    placed = (P("win", None, "wide", "narrow"), P(("win", "wide")))
    fits = mesh.shape["wide"] == 4 and mesh.shape["narrow"] == 4
    return jax.shard_map(
        two_chips if fits else any_width,
        mesh=mesh,
        in_specs=placed,
        out_specs=P(("win", "narrow"), "wide", None),
        check_vma=False,
    )
```

```python
import functools
import math

import jax
import jax.numpy as jnp
from jax import lax
from jax.experimental import pallas as pl
from jax.experimental.pallas import tpu as pltpu
from jax.sharding import PartitionSpec as P

F = 4096
L = 256
K = 4
S = 32
BINS = 128


def from_behind(array, axis, by):
    length = lax.axis_size(axis)
    pairs = [(i, i + by) for i in range(length) if 0 <= i + by < length]
    return lax.ppermute(array, axis, pairs)


def any_width(spectra, live):
    block_size = spectra.shape[2]
    bins_here = spectra.shape[3]
    wide_pos = lax.axis_index("wide")
    narrow_pos = lax.axis_index("narrow")
    high = lax.Precision.HIGHEST
    spectra_list = [spectra]
    live_list = [live]
    for offset_step in range(1, K):
        received = from_behind((spectra, live), "wide", -offset_step)
        spectra_list.append(received[0])
        live_list.append(received[1])
    partners = jnp.concatenate(spectra_list, axis=2)
    partner_live = jnp.concatenate(live_list, axis=0)
    band_size = partners.shape[2]
    real_sum = jnp.einsum("scif,scjf->ijf", spectra, partners, preferred_element_type=jnp.float32)
    imag_sum = jnp.einsum(
        "sif,sjf->ijf", spectra[:, 0], partners[:, 1], preferred_element_type=jnp.float32
    ) - jnp.einsum(
        "sif,sjf->ijf", spectra[:, 1], partners[:, 0], preferred_element_type=jnp.float32
    )
    row_ids = wide_pos * block_size + jnp.arange(block_size, dtype=jnp.int32)
    partner_ids = wide_pos * block_size + jnp.arange(band_size, dtype=jnp.int32)
    keep_mask = (
        (row_ids[:, None] != partner_ids[None, :])
        & (live[:, None] > 0)
        & (partner_live[None, :] > 0)
    ).astype(jnp.float32)
    stack_scale = keep_mask[:, :, None] / jnp.float32(math.sqrt(S))
    cross_real = (real_sum * stack_scale).astype(jnp.bfloat16)
    cross_imag = (imag_sum * stack_scale).astype(jnp.bfloat16)
    lag_shift = jnp.arange(L, dtype=jnp.int32) - L // 2
    bin_index = narrow_pos * bins_here + jnp.arange(bins_here, dtype=jnp.int32)
    phase_angle = jnp.mod(bin_index[:, None] * lag_shift[None, :], F).astype(
        jnp.float32
    ) * jnp.float32(2.0 * math.pi / F)
    cos_table = jnp.cos(phase_angle)
    sin_table = jnp.sin(phase_angle)
    summed = jnp.einsum(
        "ijf,ft->tij", cross_real, cos_table, precision=high, preferred_element_type=jnp.float32
    ) - jnp.einsum(
        "ijf,ft->tij", cross_imag, sin_table, precision=high, preferred_element_type=jnp.float32
    )
    return lax.psum_scatter(
        (summed / jnp.float32(math.sqrt(F))).astype(jnp.bfloat16),
        "narrow",
        scatter_dimension=0,
        tiled=True,
    ).astype(jnp.float32)


def correlate_kernel(crossing, starting, meta_ref, *refs):
    if crossing:
        own, near, far_a, far_b, table, before, out, acc, spread, gram = refs
        sources = (own, near, far_a, far_b)
    else:
        if starting:
            own, near, table, out, spread, gram = refs
        else:
            own, near, table, before, out, spread, gram = refs
        acc = out
        sources = (own, near)
    step = pl.program_id(0)
    points = 32 * len(sources)

    @pl.when(step == 0)
    def _():
        acc[...] = jnp.zeros_like(acc) if starting else before[...]
        if not crossing:
            spread[...] = jnp.zeros_like(spread)

    def turn(s, carry):
        for c in range(2):
            tile = jnp.concatenate([ref[s, c] for ref in sources], axis=0)
            turned = tile.astype(jnp.float32).T
            spread[pl.ds(pl.multiple_of((c * S + s) * BINS, BINS), BINS), 0:points] = turned
        return carry

    lax.fori_loop(0, S, turn, 0, unroll=4)

    def one_bin(f, carry):
        both = spread[pl.ds(f, 2 * S, stride=BINS), :]
        a, b = both[:S], both[S:]
        plain = both.astype(jnp.bfloat16)
        crossed = jnp.concatenate([b, -a], axis=0).astype(jnp.bfloat16)
        right = jnp.concatenate([plain, crossed], axis=1)
        product = lax.dot_general(
            plain[:, :32], right, (((0,), (0,)), ((), ())), preferred_element_type=jnp.float32
        )
        gram[pl.ds(pl.multiple_of(f * 32, 32), 32), :] = product[:, :128]
        gram[pl.ds(pl.multiple_of((BINS + f) * 32, 32), 32), :] = product[:, 128:]
        return carry

    lax.fori_loop(0, BINS, one_bin, 0, unroll=32)

    lane = lax.broadcasted_iota(jnp.int32, (1, 128), 1)
    sign = jnp.where((lane >= 64) & (meta_ref[1] == 1), -1.0, 1.0).astype(jnp.float32)

    def two_rows(ip, carry):
        real = [gram[pl.ds(2 * ip + r, BINS, stride=32), :] for r in range(2)]
        imag = [gram[pl.ds(BINS * 32 + 2 * ip + r, BINS, stride=32), :] * sign for r in range(2)]
        top = jnp.concatenate(real, axis=1)
        low = jnp.concatenate(imag, axis=1)
        right = jnp.concatenate([top, low], axis=0).astype(jnp.bfloat16)
        cols = pl.ds(pl.multiple_of(ip * 256, 256), 256)
        acc[:, cols] += jnp.dot(table[0], right, preferred_element_type=jnp.float32)
        return carry

    lax.fori_loop(0, 16, two_rows, 0, unroll=8)

    if crossing:
        @pl.when(step == pl.num_programs(0) - 1)
        def _():
            out[...] = (acc[...] * (1.0 / math.sqrt(S * F))).astype(out.dtype)


def correlate(meta, own, near, far, table, before, skip, chunks):
    crossing = far is not None
    block = (S, 2, 32, BINS)
    placed = pl.BlockSpec(block, lambda k, m: (0, 0, 0, m[0] + skip + k))
    near_by = pl.BlockSpec(block, lambda k, m: (0, 0, 0, skip + k))
    table_spec = pl.BlockSpec((1, L, 2 * BINS), lambda k, m: (m[0] + skip + k, 0, 0))
    whole = pl.BlockSpec((L, 4096), lambda k, m: (0, 0))
    scratch = [pltpu.VMEM((2 * S * BINS, 128), jnp.float32), pltpu.VMEM((2 * BINS * 32, 128), jnp.float32)]
    if crossing:
        in_specs = [placed, near_by, near_by, near_by, table_spec, whole]
        operands = (own, near, far[0], far[1], table, before)
        scratch = [pltpu.VMEM((L, 4096), jnp.float32)] + scratch
    else:
        in_specs = [placed, near_by, table_spec]
        operands = (own, near, table)
        if before is not None:
            in_specs.append(whole)
            operands += (before,)
    return pl.pallas_call(
        functools.partial(correlate_kernel, crossing, before is None),
        out_shape=jax.ShapeDtypeStruct((L, 4096), jnp.bfloat16 if crossing else jnp.float32),
        grid_spec=pltpu.PrefetchScalarGridSpec(
            num_scalar_prefetch=1, grid=(chunks,), in_specs=in_specs, out_specs=whole, scratch_shapes=scratch
        ),
        compiler_params=pltpu.CompilerParams(vmem_limit_bytes=48 * 2**20),
        cost_estimate=pl.CostEstimate(flops=chunks * 5 * 10**9, bytes_accessed=2**23, transcendentals=0),
    )(meta, *operands)


def fold(lags):
    return jnp.concatenate(jnp.split(lags, 4, axis=0), axis=2)


def unfold(folded):
    return jnp.concatenate(jnp.split(folded, 4, axis=2), axis=0)


def two_chips(spectra, live):
    bins_here = spectra.shape[3]
    half = bins_here // 2
    wide_pos = lax.axis_index("wide")
    narrow_pos = lax.axis_index("narrow")
    x, core = wide_pos // 2, wide_pos % 2
    over_x = [(0, 2), (1, 3), (2, 0), (3, 1)]
    on_chip = [(0, 1), (1, 0), (2, 3), (3, 2)]
    leaving = lax.dynamic_slice_in_dim(spectra, (1 - x) * half, half, 3)
    staying = lax.dynamic_slice_in_dim(spectra, x * half, half, 3)
    far_a = lax.ppermute(leaving, "wide", over_x)
    near_first = lax.ppermute(leaving, "wide", on_chip)
    near_second = lax.ppermute(staying, "wide", on_chip)
    live_near = lax.ppermute(live, "wide", on_chip)
    live_a = lax.ppermute(live, "wide", over_x)
    live_b = lax.ppermute(live_a, "wide", on_chip)

    lag_shift = jnp.arange(L, dtype=jnp.int32) - L // 2
    bin_index = narrow_pos * bins_here + jnp.arange(bins_here, dtype=jnp.int32)
    bin_index = bin_index.reshape(-1, 1, BINS)
    angle = jnp.mod(bin_index * lag_shift[None, :, None], F).astype(jnp.float32) * jnp.float32(
        2.0 * math.pi / F
    )
    table = jnp.concatenate([jnp.cos(angle), -jnp.sin(angle)], axis=2).astype(jnp.bfloat16)

    chunks = half // BINS
    first = jnp.stack([(1 - x) * chunks, x]).astype(jnp.int32)
    second = jnp.stack([x * chunks, x]).astype(jnp.int32)
    before = correlate(first, spectra, near_first, None, table, None, 0, chunks // 2)
    far_a, before = lax.optimization_barrier((far_a, before))
    far_b = lax.ppermute(far_a, "wide", on_chip)
    before = correlate(first, spectra, near_first, None, table, before, chunks // 2, chunks - chunks // 2)
    partial = correlate(second, spectra, near_second, (far_a, far_b), table, before, 0, chunks)
    mine = lax.psum_scatter(partial, "narrow", scatter_dimension=0, tiled=True)
    mine = mine.reshape(-1, 32, 128)
    back_a = unfold(lax.ppermute(fold(mine[:, :, 64:96]), "wide", [(2, 0), (3, 1)]))
    back_b = unfold(lax.ppermute(fold(mine[:, :, 96:]), "wide", [(2, 1), (3, 0)]))
    mine = mine.astype(jnp.float32)
    far_1 = mine[:, :, 64:96] + jnp.swapaxes(back_a, 1, 2).astype(jnp.float32)
    far_2 = mine[:, :, 96:] + jnp.swapaxes(back_b, 1, 2).astype(jnp.float32)
    q1 = jnp.where(core == 0, mine[:, :, 32:64], far_2)
    stacked = jnp.concatenate([mine[:, :, :32], q1, far_1, far_2], axis=2)
    row = wide_pos * 32 + jnp.arange(32, dtype=jnp.int32)
    partner = wide_pos * 32 + jnp.arange(128, dtype=jnp.int32)
    partner_live = jnp.concatenate([live, jnp.where(core == 0, live_near, live_b), live_a, live_b])
    keep = (
        (row[:, None] != partner[None, :])
        & (live[:, None] > 0)
        & (partner_live[None, :] > 0)
        & (partner[None, :] < 128)
    )
    return jnp.where(keep[None], stacked, 0.0)


def solution(mesh):
    placed = (P("win", None, "wide", "narrow"), P(("win", "wide")))
    fits = mesh.shape["wide"] == 4 and mesh.shape["narrow"] == 4
    return jax.shard_map(
        two_chips if fits else any_width,
        mesh=mesh,
        in_specs=placed,
        out_specs=P(("win", "narrow"), "wide", None),
        check_vma=False,
    )
```

```python
import functools
import math

import jax
import jax.numpy as jnp
from jax import lax
from jax.experimental import pallas as pl
from jax.experimental.pallas import tpu as pltpu
from jax.sharding import PartitionSpec as P

F = 4096
L = 256
K = 4
S = 32
BINS = 128


def from_behind(array, axis, by):
    length = lax.axis_size(axis)
    pairs = [(i, i + by) for i in range(length) if 0 <= i + by < length]
    return lax.ppermute(array, axis, pairs)


def any_width(spectra, live):
    block_size = spectra.shape[2]
    bins_here = spectra.shape[3]
    wide_pos = lax.axis_index("wide")
    narrow_pos = lax.axis_index("narrow")
    high = lax.Precision.HIGHEST
    spectra_list = [spectra]
    live_list = [live]
    for offset_step in range(1, K):
        received = from_behind((spectra, live), "wide", -offset_step)
        spectra_list.append(received[0])
        live_list.append(received[1])
    partners = jnp.concatenate(spectra_list, axis=2)
    partner_live = jnp.concatenate(live_list, axis=0)
    band_size = partners.shape[2]
    real_sum = jnp.einsum("scif,scjf->ijf", spectra, partners, preferred_element_type=jnp.float32)
    imag_sum = jnp.einsum(
        "sif,sjf->ijf", spectra[:, 0], partners[:, 1], preferred_element_type=jnp.float32
    ) - jnp.einsum(
        "sif,sjf->ijf", spectra[:, 1], partners[:, 0], preferred_element_type=jnp.float32
    )
    row_ids = wide_pos * block_size + jnp.arange(block_size, dtype=jnp.int32)
    partner_ids = wide_pos * block_size + jnp.arange(band_size, dtype=jnp.int32)
    keep_mask = (
        (row_ids[:, None] != partner_ids[None, :])
        & (live[:, None] > 0)
        & (partner_live[None, :] > 0)
    ).astype(jnp.float32)
    stack_scale = keep_mask[:, :, None] / jnp.float32(math.sqrt(S))
    cross_real = (real_sum * stack_scale).astype(jnp.bfloat16)
    cross_imag = (imag_sum * stack_scale).astype(jnp.bfloat16)
    lag_shift = jnp.arange(L, dtype=jnp.int32) - L // 2
    bin_index = narrow_pos * bins_here + jnp.arange(bins_here, dtype=jnp.int32)
    phase_angle = jnp.mod(bin_index[:, None] * lag_shift[None, :], F).astype(
        jnp.float32
    ) * jnp.float32(2.0 * math.pi / F)
    cos_table = jnp.cos(phase_angle)
    sin_table = jnp.sin(phase_angle)
    summed = jnp.einsum(
        "ijf,ft->tij", cross_real, cos_table, precision=high, preferred_element_type=jnp.float32
    ) - jnp.einsum(
        "ijf,ft->tij", cross_imag, sin_table, precision=high, preferred_element_type=jnp.float32
    )
    return lax.psum_scatter(
        (summed / jnp.float32(math.sqrt(F))).astype(jnp.bfloat16),
        "narrow",
        scatter_dimension=0,
        tiled=True,
    ).astype(jnp.float32)


def correlate_kernel(crossing, starting, meta_ref, *refs):
    if crossing:
        own, near, far_a, far_b, table, before, out, acc, spread, gram = refs
        sources = (own, near, far_a, far_b)
    else:
        if starting:
            own, near, table, out, spread, gram = refs
        else:
            own, near, table, before, out, spread, gram = refs
        acc = out
        sources = (own, near)
    step = pl.program_id(0)
    points = 32 * len(sources)

    @pl.when(step == 0)
    def _():
        acc[...] = jnp.zeros_like(acc) if starting else before[...]
        if not crossing:
            spread[...] = jnp.zeros_like(spread)

    def turn(s, carry):
        for c in range(2):
            tile = jnp.concatenate([ref[s, c] for ref in sources], axis=0)
            turned = tile.T.astype(jnp.float32)
            spread[pl.ds(pl.multiple_of((c * S + s) * BINS, BINS), BINS), 0:points] = turned
        return carry

    lax.fori_loop(0, S, turn, 0, unroll=16)

    def one_bin(f, carry):
        both = spread[pl.ds(f, 2 * S, stride=BINS), :]
        a, b = both[:S], both[S:]
        plain = both.astype(jnp.bfloat16)
        crossed = jnp.concatenate([b, -a], axis=0).astype(jnp.bfloat16)
        right = jnp.concatenate([plain, crossed], axis=1)
        product = lax.dot_general(
            plain[:, :32], right, (((0,), (0,)), ((), ())), preferred_element_type=jnp.float32
        )
        gram[pl.ds(pl.multiple_of(f * 32, 32), 32), :] = product[:, :128]
        gram[pl.ds(pl.multiple_of((BINS + f) * 32, 32), 32), :] = product[:, 128:]
        return carry

    lax.fori_loop(0, BINS, one_bin, 0, unroll=32)

    lane = lax.broadcasted_iota(jnp.int32, (1, 128), 1)
    sign = jnp.where((lane >= 64) & (meta_ref[1] == 1), -1.0, 1.0).astype(jnp.float32)

    def two_rows(ip, carry):
        real = [gram[pl.ds(2 * ip + r, BINS, stride=32), :] for r in range(2)]
        imag = [gram[pl.ds(BINS * 32 + 2 * ip + r, BINS, stride=32), :] * sign for r in range(2)]
        top = jnp.concatenate(real, axis=1)
        low = jnp.concatenate(imag, axis=1)
        right = jnp.concatenate([top, low], axis=0).astype(jnp.bfloat16)
        cols = pl.ds(pl.multiple_of(ip * 256, 256), 256)
        acc[:, cols] += jnp.dot(table[0], right, preferred_element_type=jnp.float32)
        return carry

    lax.fori_loop(0, 16, two_rows, 0, unroll=16)

    if crossing:
        @pl.when(step == pl.num_programs(0) - 1)
        def _():
            out[...] = (acc[...] * (1.0 / math.sqrt(S * F))).astype(out.dtype)


def correlate(meta, own, near, far, table, before, skip, chunks):
    crossing = far is not None
    block = (S, 2, 32, BINS)
    placed = pl.BlockSpec(block, lambda k, m: (0, 0, 0, m[0] + skip + k))
    near_by = pl.BlockSpec(block, lambda k, m: (0, 0, 0, skip + k))
    table_spec = pl.BlockSpec((1, L, 2 * BINS), lambda k, m: (m[0] + skip + k, 0, 0))
    whole = pl.BlockSpec((L, 4096), lambda k, m: (0, 0))
    scratch = [pltpu.VMEM((2 * S * BINS, 128), jnp.float32), pltpu.VMEM((2 * BINS * 32, 128), jnp.float32)]
    if crossing:
        in_specs = [placed, near_by, near_by, near_by, table_spec, whole]
        operands = (own, near, far[0], far[1], table, before)
        scratch = [pltpu.VMEM((L, 4096), jnp.float32)] + scratch
    else:
        in_specs = [placed, near_by, table_spec]
        operands = (own, near, table)
        if before is not None:
            in_specs.append(whole)
            operands += (before,)
    return pl.pallas_call(
        functools.partial(correlate_kernel, crossing, before is None),
        out_shape=jax.ShapeDtypeStruct((L, 4096), jnp.bfloat16 if crossing else jnp.float32),
        grid_spec=pltpu.PrefetchScalarGridSpec(
            num_scalar_prefetch=1, grid=(chunks,), in_specs=in_specs, out_specs=whole, scratch_shapes=scratch
        ),
        compiler_params=pltpu.CompilerParams(vmem_limit_bytes=48 * 2**20),
        cost_estimate=pl.CostEstimate(flops=chunks * 5 * 10**9, bytes_accessed=2**23, transcendentals=0),
    )(meta, *operands)


def fold(lags):
    return jnp.concatenate(jnp.split(lags, 4, axis=0), axis=2)


def unfold(folded):
    return jnp.concatenate(jnp.split(folded, 4, axis=2), axis=0)


def two_chips(spectra, live):
    bins_here = spectra.shape[3]
    half = bins_here // 2
    wide_pos = lax.axis_index("wide")
    narrow_pos = lax.axis_index("narrow")
    x, core = wide_pos // 2, wide_pos % 2
    over_x = [(0, 2), (1, 3), (2, 0), (3, 1)]
    on_chip = [(0, 1), (1, 0), (2, 3), (3, 2)]
    leaving = lax.dynamic_slice_in_dim(spectra, (1 - x) * half, half, 3)
    staying = lax.dynamic_slice_in_dim(spectra, x * half, half, 3)
    far_a = lax.ppermute(leaving, "wide", over_x)
    near_first = lax.ppermute(leaving, "wide", on_chip)
    near_second = lax.ppermute(staying, "wide", on_chip)
    live_near = lax.ppermute(live, "wide", on_chip)
    live_a = lax.ppermute(live, "wide", over_x)
    live_b = lax.ppermute(live_a, "wide", on_chip)

    lag_shift = jnp.arange(L, dtype=jnp.int32) - L // 2
    bin_index = narrow_pos * bins_here + jnp.arange(bins_here, dtype=jnp.int32)
    bin_index = bin_index.reshape(-1, 1, BINS)
    angle = jnp.mod(bin_index * lag_shift[None, :, None], F).astype(jnp.float32) * jnp.float32(
        2.0 * math.pi / F
    )
    table = jnp.concatenate([jnp.cos(angle), -jnp.sin(angle)], axis=2).astype(jnp.bfloat16)

    chunks = half // BINS
    first = jnp.stack([(1 - x) * chunks, x]).astype(jnp.int32)
    second = jnp.stack([x * chunks, x]).astype(jnp.int32)
    before = correlate(first, spectra, near_first, None, table, None, 0, chunks)
    far_a, before = lax.optimization_barrier((far_a, before))
    far_b = lax.ppermute(far_a, "wide", on_chip)
    partial = correlate(second, spectra, near_second, (far_a, far_b), table, before, 0, chunks)
    mine = lax.psum_scatter(partial, "narrow", scatter_dimension=0, tiled=True)
    mine = mine.reshape(-1, 32, 128)
    back_a = unfold(lax.ppermute(fold(mine[:, :, 64:96]), "wide", [(2, 0), (3, 1)]))
    back_b = unfold(lax.ppermute(fold(mine[:, :, 96:]), "wide", [(2, 1), (3, 0)]))
    mine = mine.astype(jnp.float32)
    far_1 = mine[:, :, 64:96] + jnp.swapaxes(back_a, 1, 2).astype(jnp.float32)
    far_2 = mine[:, :, 96:] + jnp.swapaxes(back_b, 1, 2).astype(jnp.float32)
    q1 = jnp.where(core == 0, mine[:, :, 32:64], far_2)
    stacked = jnp.concatenate([mine[:, :, :32], q1, far_1, far_2], axis=2)
    row = wide_pos * 32 + jnp.arange(32, dtype=jnp.int32)
    partner = wide_pos * 32 + jnp.arange(128, dtype=jnp.int32)
    partner_live = jnp.concatenate([live, jnp.where(core == 0, live_near, live_b), live_a, live_b])
    keep = (
        (row[:, None] != partner[None, :])
        & (live[:, None] > 0)
        & (partner_live[None, :] > 0)
        & (partner[None, :] < 128)
    )
    return jnp.where(keep[None], stacked, 0.0)


def solution(mesh):
    placed = (P("win", None, "wide", "narrow"), P(("win", "wide")))
    fits = mesh.shape["wide"] == 4 and mesh.shape["narrow"] == 4
    return jax.shard_map(
        two_chips if fits else any_width,
        mesh=mesh,
        in_specs=placed,
        out_specs=P(("win", "narrow"), "wide", None),
        check_vma=False,
    )
```

```python
import functools
import math

import jax
import jax.numpy as jnp
from jax import lax
from jax.experimental import pallas as pl
from jax.experimental.pallas import tpu as pltpu
from jax.sharding import PartitionSpec as P

F = 4096
L = 256
K = 4
S = 32
BINS = 128


def from_behind(array, axis, by):
    length = lax.axis_size(axis)
    pairs = [(i, i + by) for i in range(length) if 0 <= i + by < length]
    return lax.ppermute(array, axis, pairs)


def any_width(spectra, live):
    block_size = spectra.shape[2]
    bins_here = spectra.shape[3]
    wide_pos = lax.axis_index("wide")
    narrow_pos = lax.axis_index("narrow")
    high = lax.Precision.HIGHEST
    spectra_list = [spectra]
    live_list = [live]
    for offset_step in range(1, K):
        received = from_behind((spectra, live), "wide", -offset_step)
        spectra_list.append(received[0])
        live_list.append(received[1])
    partners = jnp.concatenate(spectra_list, axis=2)
    partner_live = jnp.concatenate(live_list, axis=0)
    band_size = partners.shape[2]
    real_sum = jnp.einsum("scif,scjf->ijf", spectra, partners, preferred_element_type=jnp.float32)
    imag_sum = jnp.einsum(
        "sif,sjf->ijf", spectra[:, 0], partners[:, 1], preferred_element_type=jnp.float32
    ) - jnp.einsum(
        "sif,sjf->ijf", spectra[:, 1], partners[:, 0], preferred_element_type=jnp.float32
    )
    row_ids = wide_pos * block_size + jnp.arange(block_size, dtype=jnp.int32)
    partner_ids = wide_pos * block_size + jnp.arange(band_size, dtype=jnp.int32)
    keep_mask = (
        (row_ids[:, None] != partner_ids[None, :])
        & (live[:, None] > 0)
        & (partner_live[None, :] > 0)
    ).astype(jnp.float32)
    stack_scale = keep_mask[:, :, None] / jnp.float32(math.sqrt(S))
    cross_real = (real_sum * stack_scale).astype(jnp.bfloat16)
    cross_imag = (imag_sum * stack_scale).astype(jnp.bfloat16)
    lag_shift = jnp.arange(L, dtype=jnp.int32) - L // 2
    bin_index = narrow_pos * bins_here + jnp.arange(bins_here, dtype=jnp.int32)
    phase_angle = jnp.mod(bin_index[:, None] * lag_shift[None, :], F).astype(
        jnp.float32
    ) * jnp.float32(2.0 * math.pi / F)
    cos_table = jnp.cos(phase_angle)
    sin_table = jnp.sin(phase_angle)
    summed = jnp.einsum(
        "ijf,ft->tij", cross_real, cos_table, precision=high, preferred_element_type=jnp.float32
    ) - jnp.einsum(
        "ijf,ft->tij", cross_imag, sin_table, precision=high, preferred_element_type=jnp.float32
    )
    return lax.psum_scatter(
        (summed / jnp.float32(math.sqrt(F))).astype(jnp.bfloat16),
        "narrow",
        scatter_dimension=0,
        tiled=True,
    ).astype(jnp.float32)


def correlate_kernel(crossing, starting, last, meta_ref, *refs):
    if crossing:
        if last:
            own, near, far_a, far_b, table, before, out, acc, spread, gram = refs
        else:
            own, near, far_a, far_b, table, before, out, spread, gram = refs
            acc = out
        sources = (own, near, far_a, far_b)
    else:
        if starting:
            own, near, table, out, spread, gram = refs
        else:
            own, near, table, before, out, spread, gram = refs
        acc = out
        sources = (own, near)
    step = pl.program_id(0)
    points = 32 * len(sources)

    @pl.when(step == 0)
    def _():
        acc[...] = jnp.zeros_like(acc) if starting else before[...]
        if not crossing:
            spread[...] = jnp.zeros_like(spread)

    def turn(s, carry):
        for c in range(2):
            tile = jnp.concatenate([ref[s, c] for ref in sources], axis=0)
            turned = tile.T.astype(jnp.float32)
            spread[pl.ds(pl.multiple_of((c * S + s) * BINS, BINS), BINS), 0:points] = turned
        return carry

    lax.fori_loop(0, S, turn, 0, unroll=16)

    def one_bin(f, carry):
        both = spread[pl.ds(f, 2 * S, stride=BINS), :]
        a, b = both[:S], both[S:]
        plain = both.astype(jnp.bfloat16)
        crossed = jnp.concatenate([b, -a], axis=0).astype(jnp.bfloat16)
        right = jnp.concatenate([plain, crossed], axis=1)
        product = lax.dot_general(
            plain[:, :32], right, (((0,), (0,)), ((), ())), preferred_element_type=jnp.float32
        )
        gram[pl.ds(pl.multiple_of(f * 32, 32), 32), :] = product[:, :128]
        gram[pl.ds(pl.multiple_of((BINS + f) * 32, 32), 32), :] = product[:, 128:]
        return carry

    lax.fori_loop(0, BINS, one_bin, 0, unroll=32)

    lane = lax.broadcasted_iota(jnp.int32, (1, 128), 1)
    sign = jnp.where((lane >= 64) & (meta_ref[1] == 1), -1.0, 1.0).astype(jnp.float32)

    def two_rows(ip, carry):
        real = [gram[pl.ds(2 * ip + r, BINS, stride=32), :] for r in range(2)]
        imag = [gram[pl.ds(BINS * 32 + 2 * ip + r, BINS, stride=32), :] * sign for r in range(2)]
        top = jnp.concatenate(real, axis=1)
        low = jnp.concatenate(imag, axis=1)
        right = jnp.concatenate([top, low], axis=0).astype(jnp.bfloat16)
        cols = pl.ds(pl.multiple_of(ip * 256, 256), 256)
        acc[:, cols] += jnp.dot(table[0], right, preferred_element_type=jnp.float32)
        return carry

    lax.fori_loop(0, 16, two_rows, 0, unroll=16)

    if last:
        @pl.when(step == pl.num_programs(0) - 1)
        def _():
            out[...] = (acc[...] * (1.0 / math.sqrt(S * F))).astype(out.dtype)


def correlate(meta, own, near, far, table, before, skip, chunks, last):
    crossing = far is not None
    block = (S, 2, 32, BINS)
    placed = pl.BlockSpec(block, lambda k, m: (0, 0, 0, m[0] + skip + k))
    near_by = pl.BlockSpec(block, lambda k, m: (0, 0, 0, skip + k))
    far_by = pl.BlockSpec(block, lambda k, m: (0, 0, 0, k))
    table_spec = pl.BlockSpec((1, L, 2 * BINS), lambda k, m: (m[0] + skip + k, 0, 0))
    whole = pl.BlockSpec((L, 4096), lambda k, m: (0, 0))
    scratch = [pltpu.VMEM((2 * S * BINS, 128), jnp.float32), pltpu.VMEM((2 * BINS * 32, 128), jnp.float32)]
    if crossing:
        in_specs = [placed, near_by, far_by, far_by, table_spec, whole]
        operands = (own, near, far[0], far[1], table, before)
        if last:
            scratch = [pltpu.VMEM((L, 4096), jnp.float32)] + scratch
    else:
        in_specs = [placed, near_by, table_spec]
        operands = (own, near, table)
        if before is not None:
            in_specs.append(whole)
            operands += (before,)
    return pl.pallas_call(
        functools.partial(correlate_kernel, crossing, before is None, last),
        out_shape=jax.ShapeDtypeStruct((L, 4096), jnp.bfloat16 if last else jnp.float32),
        grid_spec=pltpu.PrefetchScalarGridSpec(
            num_scalar_prefetch=1, grid=(chunks,), in_specs=in_specs, out_specs=whole, scratch_shapes=scratch
        ),
        compiler_params=pltpu.CompilerParams(vmem_limit_bytes=48 * 2**20),
        cost_estimate=pl.CostEstimate(flops=chunks * 5 * 10**9, bytes_accessed=2**23, transcendentals=0),
    )(meta, *operands)


def fold(lags):
    return jnp.concatenate(jnp.split(lags, 4, axis=0), axis=2)


def unfold(folded):
    return jnp.concatenate(jnp.split(folded, 4, axis=2), axis=0)


def two_chips(spectra, live):
    bins_here = spectra.shape[3]
    half = bins_here // 2
    wide_pos = lax.axis_index("wide")
    narrow_pos = lax.axis_index("narrow")
    x, core = wide_pos // 2, wide_pos % 2
    over_x = [(0, 2), (1, 3), (2, 0), (3, 1)]
    on_chip = [(0, 1), (1, 0), (2, 3), (3, 2)]
    quarter = half // 2
    early = lax.dynamic_slice_in_dim(spectra, (1 - x) * half, quarter, 3)
    far_a = lax.ppermute(early, "wide", over_x)
    early, later = lax.optimization_barrier((early, spectra))
    late = lax.dynamic_slice_in_dim(later, (1 - x) * half + quarter, quarter, 3)
    late_a = lax.ppermute(late, "wide", over_x)
    leaving = lax.dynamic_slice_in_dim(later, (1 - x) * half, half, 3)
    staying = lax.dynamic_slice_in_dim(later, x * half, half, 3)
    near_first = lax.ppermute(leaving, "wide", on_chip)
    near_second = lax.ppermute(staying, "wide", on_chip)
    live_near = lax.ppermute(live, "wide", on_chip)
    live_a = lax.ppermute(live, "wide", over_x)
    live_b = lax.ppermute(live_a, "wide", on_chip)

    lag_shift = jnp.arange(L, dtype=jnp.int32) - L // 2
    bin_index = narrow_pos * bins_here + jnp.arange(bins_here, dtype=jnp.int32)
    bin_index = bin_index.reshape(-1, 1, BINS)
    angle = jnp.mod(bin_index * lag_shift[None, :, None], F).astype(jnp.float32) * jnp.float32(
        2.0 * math.pi / F
    )
    table = jnp.concatenate([jnp.cos(angle), -jnp.sin(angle)], axis=2).astype(jnp.bfloat16)

    chunks = half // BINS
    first = jnp.stack([(1 - x) * chunks, x]).astype(jnp.int32)
    second = jnp.stack([x * chunks, x]).astype(jnp.int32)
    before = correlate(first, spectra, near_first, None, table, None, 0, chunks, False)
    far_a, before = lax.optimization_barrier((far_a, before))
    far_b = lax.ppermute(far_a, "wide", on_chip)
    part = chunks // 2
    before = correlate(second, spectra, near_second, (far_a, far_b), table, before, 0, part, False)
    late_a, before = lax.optimization_barrier((late_a, before))
    late_b = lax.ppermute(late_a, "wide", on_chip)
    partial = correlate(
        second, spectra, near_second, (late_a, late_b), table, before, part, chunks - part, True
    )
    mine = lax.psum_scatter(partial, "narrow", scatter_dimension=0, tiled=True)
    mine = mine.reshape(-1, 32, 128)
    back_a = unfold(lax.ppermute(fold(mine[:, :, 64:96]), "wide", [(2, 0), (3, 1)]))
    back_b = unfold(lax.ppermute(fold(mine[:, :, 96:]), "wide", [(2, 1), (3, 0)]))
    mine = mine.astype(jnp.float32)
    far_1 = mine[:, :, 64:96] + jnp.swapaxes(back_a, 1, 2).astype(jnp.float32)
    far_2 = mine[:, :, 96:] + jnp.swapaxes(back_b, 1, 2).astype(jnp.float32)
    q1 = jnp.where(core == 0, mine[:, :, 32:64], far_2)
    stacked = jnp.concatenate([mine[:, :, :32], q1, far_1, far_2], axis=2)
    row = wide_pos * 32 + jnp.arange(32, dtype=jnp.int32)
    partner = wide_pos * 32 + jnp.arange(128, dtype=jnp.int32)
    partner_live = jnp.concatenate([live, jnp.where(core == 0, live_near, live_b), live_a, live_b])
    keep = (
        (row[:, None] != partner[None, :])
        & (live[:, None] > 0)
        & (partner_live[None, :] > 0)
        & (partner[None, :] < 128)
    )
    return jnp.where(keep[None], stacked, 0.0)


def solution(mesh):
    placed = (P("win", None, "wide", "narrow"), P(("win", "wide")))
    fits = mesh.shape["wide"] == 4 and mesh.shape["narrow"] == 4
    return jax.shard_map(
        two_chips if fits else any_width,
        mesh=mesh,
        in_specs=placed,
        out_specs=P(("win", "narrow"), "wide", None),
        check_vma=False,
    )
```
